128 devices in a mesh: sx: 16 (over y_hi, x, core), sy: 8 (over z, y_lo).
Axes of the slice: x: 4, y: 4 (y_hi: 2, y_lo: 2; y = y_hi * 2 + y_lo), z: 4, core: 2. Of those that a mesh axis runs over, the one named last changes fastest.
Arguments:
- weights: bfloat16 [2048, 1024, 128], P('sx', 'sy'), may hold values from -6 to 6
- velocity: bfloat16 [2048, 1024], P('sx', 'sy'), may hold values from 0.5 to 3
- translation: bfloat16 [2, 2, 2, 2, 64, 64], replicated, may hold values from -0.375 to 0.375
Outputs:
- final_weights: float32 [2048, 1024, 128], P('sx', 'sy')
The draws below stay inside these ranges and needn't reach their ends.
All inputs are finite; a program needn't handle non-finite values.
Results may differ from the reference program's by a relative error of at most 0.0081.
Values may be sent and summed in bfloat16 or wider, within the bound.
No kernel may reach another device: no remote copies, remote signals or barrier semaphores. Data moves between devices by JAX's collectives and lax.ppermute only.
A program may use at most 128 MiB of HBM per device.

```python
import math
import jax
import jax.numpy as jnp

RANK = 64
LEVELS = 8
NX = 2048
NY = 1024


def shard_levels(own_key, shape, split, smallest, high):
    def one(position, shards_of):
        heights = jax.random.uniform(jax.random.fold_in(jax.random.fold_in(own_key, 6), position), (shards_of,), jnp.float32, smallest / len(split), high / len(split))
        return jnp.repeat(jnp.exp(heights), shape[position] // shards_of).reshape((-1,) + (1,) * (len(shape) - position - 1))

    gain = one(*split[0])
    for cut in split[1:]:
        gain = gain * one(*cut)
    return gain


def scatter_about(rng, shape, spread, most, pieces=(), kind=jnp.bfloat16):
    drawn = jax.random.normal(rng, shape, jnp.float32) * spread
    if len(pieces) > 0:
        drawn = shard_levels(rng, shape, pieces, -0.22, 0.18) * drawn
    return jnp.clip(drawn, min=-most, max=most).astype(kind)


def setup_inputs(seed: int = 0) -> dict:
    streams_of = jax.random.split(jax.random.key(seed), 4)
    return {
        "weights": scatter_about(streams_of[0], (NX, NY, 2 * RANK), 1.0, 6.0, ((0, 16), (1, 8))),
        "velocity": jnp.clip(jnp.exp(math.log(3.0) - 1.7917595 * jax.random.uniform(streams_of[1], (NX, NY), jnp.float32) ** shard_levels(streams_of[1], (NX, NY), ((0, 16), (1, 8)), -0.2, 0.2)), 0.5, 3.0).astype(jnp.bfloat16),
        "translation": scatter_about(streams_of[2], (2, 2, 2, 2, RANK, RANK), (4 * RANK) ** -0.5, 0.375),
    }


def node_totals():
    counter = jnp.arange(8, dtype=jnp.float32)
    nodes = jnp.cos(jnp.pi * (2.0 * counter + 1.0) / 16.0)
    return (nodes[:, None] + nodes[None, :]).reshape(64)


def phase_angles(velocity, level_index):
    totals = node_totals()
    return (velocity.astype(jnp.float32)[..., None] * totals) * (0.5 * (level_index + 1))


def rotate_phase(values, angles, sign):
    cosine = jnp.cos(angles)
    sine = sign * jnp.sin(angles)
    real_part = values[..., :64]
    imag_part = values[..., 64:]
    return jnp.concatenate([real_part * cosine - imag_part * sine, real_part * sine + imag_part * cosine], axis=-1)


def block_matrices(translation, dim_index):
    blocks = translation[dim_index]
    upper = jnp.concatenate([blocks[:, :, 0], blocks[:, :, 1]], axis=-1)
    lower = jnp.concatenate([-blocks[:, :, 1], blocks[:, :, 0]], axis=-1)
    return jnp.concatenate([upper, lower], axis=-2)


def combine_pairs(first, second, matrices):
    outputs = []
    for target in range(2):
        term = jnp.dot(first, matrices[target, 0], preferred_element_type=jnp.float32)
        outputs.append(term + jnp.dot(second, matrices[target, 1], preferred_element_type=jnp.float32))
    return outputs


def reference(weights, velocity, translation):
    state = weights.astype(jnp.float32)
    width = 2 * RANK
    for level_index in range(LEVELS):
        dim_index = level_index % 2
        depth = level_index // 2
        angles = phase_angles(velocity, level_index)
        mixed = rotate_phase(state, angles, -1.0).astype(jnp.bfloat16)
        matrices = block_matrices(translation, dim_index)
        if dim_index == 0:
            distance = NX >> (depth + 1)
            grouped = mixed.reshape(NX // (2 * distance), 2, distance, NY, width)
            outputs = combine_pairs(grouped[:, 0], grouped[:, 1], matrices)
            joined = jnp.stack(outputs, axis=1).reshape(NX, NY, width)
        else:
            distance = NY >> (depth + 1)
            grouped = mixed.reshape(NX, NY // (2 * distance), 2, distance, width)
            outputs = combine_pairs(grouped[:, :, 0], grouped[:, :, 1], matrices)
            joined = jnp.stack(outputs, axis=2).reshape(NX, NY, width)
        state = rotate_phase(joined, angles, 1.0)
    return state
```

```python
import functools

import jax
import jax.numpy as jnp
import numpy as np
from jax import lax
from jax.experimental import pallas as pl
from jax.experimental.pallas import tpu as pltpu
from jax.sharding import PartitionSpec as P

CHUNKS = 2
TERMS = 7
MAX_ANGLE = 2.95
EVERY = ("sx", "sy")


def level_bits(count_x, count_y):
    bits_x = count_x.bit_length() - 1
    bits_y = count_y.bit_length() - 1
    order = []
    for step in range(4):
        order.append(bits_y + bits_x - 1 - step)
        order.append(bits_y - 1 - step if step < bits_y else None)
    return order


def half_totals():
    counter = np.arange(8, dtype=np.float64)
    nodes = np.cos(np.pi * (2.0 * counter + 1.0) / 16.0)
    totals = (nodes[:, None] + nodes[None, :]).reshape(64) * 0.5
    return np.concatenate([totals, totals])


def trig_constants():
    top = MAX_ANGLE**2
    count = 400
    square = (np.cos(np.pi * (np.arange(count) + 0.5) / count) + 1) / 2 * top
    angle = np.sqrt(square)

    def fit(values):
        series = np.polynomial.chebyshev.Chebyshev.fit(square, values, TERMS - 1, domain=[0, top])
        return series.convert(kind=np.polynomial.Polynomial, domain=[-1, 1], window=[-1, 1]).coef

    rows = np.zeros((TERMS + 1, 128), np.float32)
    rows[:TERMS, :64] = fit(np.cos(angle))[:, None]
    rows[:TERMS, 64:] = fit(np.sin(angle) / angle)[:, None]
    rows[TERMS] = half_totals()
    return rows


def swap_parts(values):
    return pltpu.roll(values, 64, values.ndim - 1)


def trig_kernel(const_ref, velocity_ref, trig_ref, *, group):
    sources, half, _ = trig_ref.shape[0], trig_ref.shape[2], 0
    rows = 2 * half
    low_row = pl.program_id(0) * half
    lane = lax.broadcasted_iota(jnp.int32, (rows * group, 128), 1)
    row = lax.broadcasted_iota(jnp.int32, (rows * group, 128), 0) % rows
    diagonal = lane == jnp.where(row < half, row, row - half + 64) + low_row
    ones = jnp.ones((128, 128), jnp.bfloat16)

    def step(index, carry):
        first = index * group
        spread = jnp.concatenate(
            [jnp.broadcast_to(velocity_ref[pl.ds(first + j, 1), :], (rows, 128)) for j in range(group)], 0
        )
        picked = jnp.where(diagonal, spread, 0.0).astype(jnp.bfloat16)
        speed = jnp.dot(picked, ones, preferred_element_type=jnp.float32)
        angle = speed * const_ref[TERMS : TERMS + 1, :]
        square = angle * angle
        series = jnp.broadcast_to(const_ref[TERMS - 1 : TERMS, :], square.shape)
        for k in range(TERMS - 2, -1, -1):
            series = series * square + const_ref[k : k + 1, :]
        both = series * jnp.where(lane < 64, 1.0, angle)
        trig_ref[pl.ds(first, group)] = both.reshape(group, 2, half, 128)
        return carry

    lax.fori_loop(0, sources // group, step, 0)


def trig_table(velocity, half=16, group=32):
    sources = velocity.shape[0]
    const = jnp.asarray(trig_constants())
    return pl.pallas_call(
        functools.partial(trig_kernel, group=group),
        grid=(64 // half,),
        in_specs=[
            pl.BlockSpec(const.shape, lambda g: (0, 0)),
            pl.BlockSpec(velocity.shape, lambda g: (0, 0)),
        ],
        out_specs=pl.BlockSpec((sources, 2, half, 128), lambda g: (0, 0, g, 0)),
        out_shape=jax.ShapeDtypeStruct((sources, 2, 64, 128), jnp.float32),
        compiler_params=pltpu.CompilerParams(vmem_limit_bytes=24 * 2**20),
        cost_estimate=pl.CostEstimate(flops=4 * 10**9, bytes_accessed=8 * 2**20, transcendentals=0),
    )(const, velocity)


def butterfly_kernel(weights_x, weights_y, trig_ref, in_ref, out_ref, cos_ref, sin_ref, state_ref, *, bits, group):
    sources, _, half, _ = in_ref.shape
    rows = 2 * half
    low = lax.broadcasted_iota(jnp.int32, (group * rows, 128), 1) < 64

    def enter(index, carry):
        first = index * group
        both = trig_ref[pl.ds(first, group)].reshape(group * rows, 128)
        other = swap_parts(both)
        cosine = jnp.where(low, both, other)
        sine = jnp.where(low, other, -both)
        values = in_ref[pl.ds(first, group)].reshape(group * rows, 128).astype(jnp.float32)
        turned = values * cosine + swap_parts(values) * sine
        cos_ref[pl.ds(first, group)] = cosine.reshape(group, rows, 128)
        sin_ref[pl.ds(first, group)] = sine.reshape(group, rows, 128)
        state_ref[pl.ds(first, group)] = turned.astype(jnp.bfloat16).reshape(group, rows, 128)
        return carry

    lax.fori_loop(0, sources // group, enter, 0)

    for level, bit in enumerate(bits):
        matrix = (weights_x, weights_y)[level % 2]
        if bit is not None:
            pairs = []
            for pair in range(sources // 2):
                lower = (pair >> bit) << (bit + 1) | pair & (1 << bit) - 1
                pairs.append((lower, lower + (1 << bit)))
            left = jnp.concatenate([jnp.concatenate([state_ref[a], state_ref[b]], 1) for a, b in pairs], 0)
            joined = jnp.dot(left, matrix[...], preferred_element_type=jnp.float32)
            for place, pair in enumerate(pairs):
                for side, box in enumerate(pair):
                    values = joined[place * rows : (place + 1) * rows, side * 128 : side * 128 + 128]
                    turned = values * cos_ref[box] + swap_parts(values) * sin_ref[box]
                    state_ref[box] = turned.astype(jnp.bfloat16)
        else:
            left = jnp.concatenate(
                [jnp.concatenate([state_ref[a, :half], state_ref[a, half:]], 1) for a in range(sources)], 0
            )
            joined = jnp.dot(left, matrix[...], preferred_element_type=jnp.float32)
            for box in range(sources):
                cosine, sine = cos_ref[box], sin_ref[box]
                for _ in range(3):
                    cosine, sine = cosine * cosine - sine * sine, 2.0 * (cosine * sine)
                part = joined[box * half : (box + 1) * half]
                values = jnp.concatenate([part[:, :128], part[:, 128:]], 0)
                turned = values * cosine - swap_parts(values) * sine
                out_ref[box] = turned.astype(out_ref.dtype).reshape(2, half, 128)


def butterfly(values, trig, matrix_x, matrix_y, chunk, bits, half=16, group=16):
    sources, _, extent, _ = values.shape
    first = chunk * extent // half
    whole = pl.BlockSpec((256, 256), lambda g: (0, 0))
    block = pl.BlockSpec((sources, 2, half, 128), lambda g: (0, 0, g, 0))
    trig_block = pl.BlockSpec((sources, 2, half, 128), lambda g: (0, 0, first + g, 0))
    table = pltpu.VMEM((sources, 2 * half, 128), jnp.float32)
    return pl.pallas_call(
        functools.partial(butterfly_kernel, bits=bits, group=group),
        grid=(extent // half,),
        in_specs=[whole, whole, trig_block, block],
        out_specs=block,
        out_shape=jax.ShapeDtypeStruct(values.shape, jnp.bfloat16),
        scratch_shapes=[table, table, pltpu.VMEM((sources, 2 * half, 128), jnp.bfloat16)],
        compiler_params=pltpu.CompilerParams(vmem_limit_bytes=48 * 2**20),
        cost_estimate=pl.CostEstimate(
            flops=16 * 10**9 * extent // 64, bytes_accessed=16 * 2**20 * extent // 64, transcendentals=0
        ),
    )(matrix_x, matrix_y, trig, values)


def pair_matrix(translation, dim_index):
    blocks = translation[dim_index]
    upper = jnp.concatenate([blocks[:, :, 0], blocks[:, :, 1]], axis=-1)
    lower = jnp.concatenate([-blocks[:, :, 1], blocks[:, :, 0]], axis=-1)
    matrices = jnp.concatenate([upper, lower], axis=-2)
    return matrices.transpose(1, 2, 0, 3).reshape(256, 256)


def exchange(values):
    return lax.all_to_all(values, EVERY, 0, 0, tiled=True)


def shards(weights, velocity, translation):
    bits = level_bits(lax.axis_size("sx"), lax.axis_size("sy"))
    grouped = weights.reshape(128, 2, 64, 128)
    size = 64 // CHUNKS
    speeds = exchange(velocity[:, None, :]).reshape(128, 128).astype(jnp.float32)
    trig = trig_table(speeds)
    matrix_x = pair_matrix(translation, 0)
    matrix_y = pair_matrix(translation, 1)
    results = []
    for chunk in range(CHUNKS):
        arrived = exchange(grouped[:, :, chunk * size : (chunk + 1) * size])
        results.append(exchange(butterfly(arrived, trig, matrix_x, matrix_y, chunk, bits)))
    final = jnp.concatenate([part.astype(jnp.float32) for part in results], axis=2)
    return final.reshape(128, 128, 128)


def solution(mesh):
    placed = (P("sx", "sy", None), P("sx", "sy"), P())
    return jax.shard_map(
        shards, mesh=mesh, in_specs=placed, out_specs=P("sx", "sy", None), check_vma=False
    )
```

```python
import functools

import jax
import jax.numpy as jnp
import numpy as np
from jax import lax
from jax.experimental import pallas as pl
from jax.experimental.pallas import tpu as pltpu
from jax.sharding import PartitionSpec as P

TERMS = 7
MAX_ANGLE = 2.95
HALF = 16
EVERY = ("sx", "sy")
CHUNKS = 2
STRIPS = 2
VMEM_LIMIT = 60 * 2**20


def unit_bits(count_x, count_y):
    bits_x = count_x.bit_length() - 1
    bits_y = count_y.bit_length() - 1
    order = []
    for step in range(bits_x):
        order.append(bits_y + bits_x - step)
        order.append(bits_y - step)
    return order


def half_totals():
    counter = np.arange(8, dtype=np.float64)
    nodes = np.cos(np.pi * (2.0 * counter + 1.0) / 16.0)
    totals = (nodes[:, None] + nodes[None, :]).reshape(64) * 0.5
    return np.concatenate([totals, totals])


def trig_constants():
    top = MAX_ANGLE**2
    count = 400
    square = (np.cos(np.pi * (np.arange(count) + 0.5) / count) + 1) / 2 * top
    angle = np.sqrt(square)

    def fit(values):
        series = np.polynomial.chebyshev.Chebyshev.fit(square, values, TERMS - 1, domain=[0, top])
        return series.convert(kind=np.polynomial.Polynomial, domain=[-1, 1], window=[-1, 1]).coef

    rows = np.zeros((TERMS + 1, 128), np.float32)
    rows[:TERMS, :64] = fit(np.cos(angle))[:, None]
    rows[:TERMS, 64:] = fit(np.sin(angle) / angle)[:, None]
    rows[TERMS] = half_totals()
    return rows


def spread_index(place, bit):
    return (place >> bit) << (bit + 1) | place & (1 << bit) - 1


def drop_bit(unit, bit):
    return (unit >> (bit + 1)) << bit | unit & (1 << bit) - 1


def butterfly_kernel(
    const_ref, speed_ref, split_ref, matrix_x, matrix_y, *refs, bits, wide, group, start
):
    in_refs, out_ref, plain_ref, swapped_ref, states = refs[:2], refs[2], refs[3], refs[4], refs[5:]
    sources, extent, _ = in_refs[0].shape
    half = HALF
    strips = range(extent // half)
    units = 2 * sources
    low = lax.broadcasted_iota(jnp.int32, (half, 128), 1) < 64

    first_row = start + pl.program_id(0) * extent
    lane = lax.broadcasted_iota(jnp.int32, (2 * extent * group, 128), 1)
    row = lax.broadcasted_iota(jnp.int32, (2 * extent * group, 128), 0) % (2 * extent)
    diagonal = lane == jnp.where(row < extent, row, row - extent + 64) + first_row
    ones = jnp.ones((128, 128), jnp.bfloat16)

    def trig(index, carry):
        first = index * group
        spread = jnp.concatenate(
            [jnp.broadcast_to(speed_ref[pl.ds(first + j, 1), :], (2 * extent, 128)) for j in range(group)], 0
        )
        picked = jnp.where(diagonal, spread, 0.0).astype(jnp.bfloat16)
        speed = jnp.dot(picked, ones, preferred_element_type=jnp.float32)
        angle = speed * const_ref[TERMS : TERMS + 1, :]
        square = angle * angle
        series = jnp.broadcast_to(const_ref[TERMS - 1 : TERMS, :], square.shape)
        for k in range(TERMS - 2, -1, -1):
            series = series * square + const_ref[k : k + 1, :]
        both = series * jnp.where(lane < 64, 1.0, angle)
        plain_ref[pl.ds(2 * first, 2 * group)] = both.reshape(2 * group, extent, 128)
        swapped_ref[pl.ds(2 * first, 2 * group)] = pltpu.roll(both, 64, 1).reshape(2 * group, extent, 128)
        return carry

    lax.fori_loop(0, units // 2 // group, trig, 0)

    def tables(first, second, rows):
        cosine = jnp.where(low, plain_ref[first, rows], swapped_ref[second, rows])
        sine = jnp.where(low, swapped_ref[first, rows], plain_ref[second, rows])
        return cosine, sine

    def emit(chosen, left, matrix, finish):
        for begin in range(0, len(chosen), wide):
            joined = jnp.dot(
                jnp.concatenate(left[begin : begin + wide], 0), matrix, preferred_element_type=jnp.float32
            )
            for k, pair in enumerate(chosen[begin : begin + wide]):
                part = joined[k * half : (k + 1) * half]
                finish(pair, part[:, :128], part[:, 128:])

    def turn_back(target, place, rows, real, imag, cosine, sine):
        re_ref, im_ref = target
        re_ref[place, rows] = (real * cosine + imag * sine).astype(jnp.bfloat16)
        im_ref[place, rows] = (imag * cosine - real * sine).astype(jnp.bfloat16)

    pairs = [(spread_index(p, bits[0]), spread_index(p, bits[0]) + (1 << bits[0])) for p in range(units // 2)]
    for strip in strips:
        rows = slice(strip * half, (strip + 1) * half)
        left = [
            jnp.concatenate([in_refs[a % 2][a // 2, rows], in_refs[b % 2][b // 2, rows]], 1) for a, b in pairs
        ]

        def enter(pair, real, imag, rows=rows):
            turn_back(states[:2], drop_bit(pair[0], bits[0]), rows, real, imag, *tables(*pair, rows))

        emit(pairs, left, split_ref[...], enter)

    for level, bit in enumerate(bits):
        before = bits[level - 1] if level else None
        after = bits[level + 1] if level + 1 < len(bits) else None
        now, later = states[2 * (level % 2) :][:2], states[2 * ((level + 1) % 2) :][:2]
        for strip in strips:
            rows = slice(strip * half, (strip + 1) * half)
            for was in range(2 if level else 1):
                for will in range(2 if after is not None else 1):
                    chosen, left = [], []
                    for p in range(units // 2):
                        a = spread_index(p, bit)
                        b = a + (1 << bit)
                        if before is not None and (a >> before) & 1 != was:
                            continue
                        if after is not None and (a >> after) & 1 != will:
                            continue
                        chosen.append((a, b))
                        if before is None:
                            left.append(jnp.concatenate([now[0][p, rows], now[1][p, rows]], 1))
                        else:
                            i, j = drop_bit(a, before), drop_bit(b, before)
                            if was:
                                i, j = j, i
                            left.append(
                                jnp.concatenate([jnp.where(low, part[i, rows], part[j, rows]) for part in now], 1)
                            )

                    def leave(pair, real, imag, rows=rows, will=will, bit=bit, after=after, later=later):
                        a, b = pair
                        cosine, sine = tables(b, a, rows) if will else tables(a, b, rows)
                        if after is not None:
                            turn_back(later, drop_bit(a, bit), rows, real, imag, cosine, sine)
                            return
                        for _ in range(3):
                            cosine, sine = cosine * cosine - sine * sine, 2.0 * (cosine * sine)
                        out_ref[a // 2, 0, rows] = (real * cosine - imag * sine).astype(jnp.bfloat16)
                        out_ref[a // 2, 1, rows] = (imag * cosine + real * sine).astype(jnp.bfloat16)

                    emit(chosen, left, (matrix_x, matrix_y)[level % 2][was, will], leave)


def butterfly(values, speed, start, extent, split, matrices, bits, wide=32, strips=STRIPS, group=16):
    sources = values.shape[0]
    size = strips * HALF
    blocks = extent // size
    const = jnp.asarray(trig_constants())
    inputs = [
        pl.BlockSpec((sources, size, 128), lambda g, part=part: (0, part * blocks + g, 0)) for part in range(2)
    ]
    state = pltpu.VMEM((sources, size, 128), jnp.bfloat16)
    table = pltpu.VMEM((2 * sources, size, 128), jnp.float32)
    return pl.pallas_call(
        functools.partial(butterfly_kernel, bits=bits, wide=wide, group=group, start=start),
        grid=(blocks,),
        in_specs=[
            pl.BlockSpec(const.shape, lambda g: (0, 0)),
            pl.BlockSpec(speed.shape, lambda g: (0, 0)),
            pl.BlockSpec(split.shape, lambda g: (0, 0)),
            pl.BlockSpec((2, 2, 256, 256), lambda g: (0, 0, 0, 0)),
            pl.BlockSpec((2, 2, 256, 256), lambda g: (0, 0, 0, 0)),
            *inputs,
        ],
        out_specs=pl.BlockSpec((sources, 2, size, 128), lambda g: (0, 0, g, 0)),
        out_shape=jax.ShapeDtypeStruct((sources, 2, extent, 128), jnp.bfloat16),
        scratch_shapes=[table, table] + [state] * 4,
        compiler_params=pltpu.CompilerParams(vmem_limit_bytes=VMEM_LIMIT),
        cost_estimate=pl.CostEstimate(
            flops=14 * 10**9 * extent // 64, bytes_accessed=8 * 2**20 * extent // 64, transcendentals=0
        ),
    )(const, speed, split, *matrices, values, values)


def finish_kernel(in_ref, *refs):
    out_ref = refs[-1]
    low = lax.broadcasted_iota(jnp.int32, (1, 128), 1) < 64
    for j in range(out_ref.shape[0]):
        real, imag = in_ref[j, 0].astype(jnp.float32), in_ref[j, 1].astype(jnp.float32)
        out_ref[j, 0] = jnp.where(low, real, pltpu.roll(imag, 64, 1))
        out_ref[j, 1] = jnp.where(low, pltpu.roll(real, 64, 1), imag)


def finish(values, chunk, output, group=32):
    boxes, _, extent, _ = values.shape
    earlier = [] if output is None else [output]
    return pl.pallas_call(
        finish_kernel,
        grid=(boxes // group,),
        in_specs=[pl.BlockSpec((group, 2, extent, 128), lambda g: (g, 0, 0, 0))]
        + [pl.BlockSpec(memory_space=pl.ANY)] * len(earlier),
        out_specs=pl.BlockSpec((group, 2, extent, 128), lambda g: (g, 0, chunk, 0)),
        out_shape=jax.ShapeDtypeStruct((boxes, 2, CHUNKS * extent, 128), jnp.float32),
        input_output_aliases={1: 0} if earlier else {},
        compiler_params=pltpu.CompilerParams(vmem_limit_bytes=24 * 2**20),
        cost_estimate=pl.CostEstimate(flops=10**7, bytes_accessed=6 * 2**20, transcendentals=0),
    )(values, *earlier)


def pair_matrices(translation):
    real, imag = translation[:, :, 0], translation[:, :, 1]
    blocks = jnp.stack([jnp.stack([real, imag]), jnp.stack([-imag, real])])
    blocks = blocks.transpose(0, 3, 4, 1, 2, 5)
    rows = jnp.stack([blocks, blocks[:, ::-1]])
    both = jnp.stack([rows, rows[:, :, :, :, :, ::-1]], 1)
    return both.reshape(2, 2, 256, 256)


def split_matrix():
    out = np.zeros((256, 256), np.float32)
    for box in range(2):
        for part in range(2):
            for t in range(64):
                out[box * 128 + part * 64 + t, part * 128 + box * 64 + t] = 1
    return jnp.asarray(out, jnp.bfloat16)


def exchange(values):
    return lax.all_to_all(values, EVERY, 0, 0, tiled=True)


def shards(weights, velocity, translation):
    bits = unit_bits(lax.axis_size("sx"), lax.axis_size("sy"))
    boxes = weights.shape[0]
    size = 64 // CHUNKS
    rows = 2 * size
    grouped = weights.reshape(boxes, 2, CHUNKS, size, 128)
    split = split_matrix()
    matrices = [pair_matrices(translation[dim]) for dim in range(2)]
    extra = jnp.broadcast_to(velocity[:, None], (boxes, 8, 128))
    first = grouped[:, :, 0].reshape(boxes, rows, 128)
    arrived = [exchange(jnp.concatenate([first, extra], 1))]
    second = grouped[:, :, 1].reshape(boxes, rows, 128)
    arrived[0], second, matrices, split = lax.optimization_barrier((arrived[0], second, matrices, split))
    arrived.append(exchange(second))
    speed = arrived[0][:, rows].astype(jnp.float32)
    back = []
    for chunk in range(CHUNKS):
        done = butterfly(arrived[chunk], speed, chunk * size, size, split, matrices, bits)
        back.append(exchange(done))
    output = None
    for chunk in range(CHUNKS):
        if chunk:
            back[chunk], output = lax.optimization_barrier((back[chunk], output))
        output = finish(back[chunk], chunk, output)
    return output.reshape(weights.shape)


def solution(mesh):
    placed = (P("sx", "sy", None), P("sx", "sy"), P())
    return jax.shard_map(
        shards, mesh=mesh, in_specs=placed, out_specs=P("sx", "sy", None), check_vma=False
    )
```

```python
import functools

import jax
import jax.numpy as jnp
import numpy as np
from jax import lax
from jax.experimental import pallas as pl
from jax.experimental.pallas import tpu as pltpu
from jax.sharding import PartitionSpec as P

TERMS = 7
MAX_ANGLE = 2.95
HALF = 16
EVERY = ("sx", "sy")
CHUNKS = 2
STRIPS = 2
VMEM_LIMIT = 60 * 2**20


def unit_bits(count_x, count_y):
    bits_x = count_x.bit_length() - 1
    bits_y = count_y.bit_length() - 1
    order = []
    for step in range(bits_x):
        order.append(bits_y + bits_x - step)
        order.append(bits_y - step)
    return order


def half_totals():
    counter = np.arange(8, dtype=np.float64)
    nodes = np.cos(np.pi * (2.0 * counter + 1.0) / 16.0)
    totals = (nodes[:, None] + nodes[None, :]).reshape(64) * 0.5
    return np.concatenate([totals, totals])


def trig_constants():
    top = MAX_ANGLE**2
    count = 400
    square = (np.cos(np.pi * (np.arange(count) + 0.5) / count) + 1) / 2 * top
    angle = np.sqrt(square)

    def fit(values):
        series = np.polynomial.chebyshev.Chebyshev.fit(square, values, TERMS - 1, domain=[0, top])
        return series.convert(kind=np.polynomial.Polynomial, domain=[-1, 1], window=[-1, 1]).coef

    rows = np.zeros((TERMS + 1, 128), np.float32)
    rows[:TERMS, :64] = fit(np.cos(angle))[:, None]
    rows[:TERMS, 64:] = fit(np.sin(angle) / angle)[:, None]
    rows[TERMS] = half_totals()
    return rows


def spread_index(place, bit):
    return (place >> bit) << (bit + 1) | place & (1 << bit) - 1


def drop_bit(unit, bit):
    return (unit >> (bit + 1)) << bit | unit & (1 << bit) - 1


def butterfly_kernel(
    const_ref, speed_ref, split_ref, matrix_x, matrix_y, *refs, bits, wide, group, start
):
    in_refs, out_ref, plain_ref, swapped_ref, states = refs[:2], refs[2], refs[3], refs[4], refs[5:]
    sources, extent, _ = in_refs[0].shape
    half = HALF
    strips = range(extent // half)
    units = 2 * sources
    low = lax.broadcasted_iota(jnp.int32, (half, 128), 1) < 64

    first_row = start + pl.program_id(0) * extent
    lane = lax.broadcasted_iota(jnp.int32, (2 * extent * group, 128), 1)
    row = lax.broadcasted_iota(jnp.int32, (2 * extent * group, 128), 0) % (2 * extent)
    diagonal = lane == jnp.where(row < extent, row, row - extent + 64) + first_row
    ones = jnp.ones((128, 128), jnp.bfloat16)

    def trig(index, carry):
        first = index * group
        spread = jnp.concatenate(
            [jnp.broadcast_to(speed_ref[pl.ds(first + j, 1), :], (2 * extent, 128)) for j in range(group)], 0
        )
        picked = jnp.where(diagonal, spread, 0.0).astype(jnp.bfloat16)
        speed = jnp.dot(picked, ones, preferred_element_type=jnp.float32)
        angle = speed * const_ref[TERMS : TERMS + 1, :]
        square = angle * angle
        series = jnp.broadcast_to(const_ref[TERMS - 1 : TERMS, :], square.shape)
        for k in range(TERMS - 2, -1, -1):
            series = series * square + const_ref[k : k + 1, :]
        both = series * jnp.where(lane < 64, 1.0, angle)
        plain_ref[pl.ds(2 * first, 2 * group)] = both.reshape(2 * group, extent, 128)
        swapped_ref[pl.ds(2 * first, 2 * group)] = pltpu.roll(both, 64, 1).reshape(2 * group, extent, 128)
        return carry

    lax.fori_loop(0, units // 2 // group, trig, 0)

    def tables(first, second, rows):
        cosine = jnp.where(low, plain_ref[first, rows], swapped_ref[second, rows])
        sine = jnp.where(low, swapped_ref[first, rows], plain_ref[second, rows])
        return cosine, sine

    def emit(chosen, left, matrix, finish):
        for begin in range(0, len(chosen), wide):
            joined = jnp.dot(
                jnp.concatenate(left[begin : begin + wide], 0), matrix, preferred_element_type=jnp.float32
            )
            for k, pair in enumerate(chosen[begin : begin + wide]):
                part = joined[k * half : (k + 1) * half]
                finish(pair, part[:, :128], part[:, 128:])

    def turn_back(target, place, rows, real, imag, cosine, sine):
        re_ref, im_ref = target
        re_ref[place, rows] = (real * cosine + imag * sine).astype(jnp.bfloat16)
        im_ref[place, rows] = (imag * cosine - real * sine).astype(jnp.bfloat16)

    pairs = [(spread_index(p, bits[0]), spread_index(p, bits[0]) + (1 << bits[0])) for p in range(units // 2)]
    for strip in strips:
        rows = slice(strip * half, (strip + 1) * half)
        left = [
            jnp.concatenate([in_refs[a % 2][a // 2, rows], in_refs[b % 2][b // 2, rows]], 1) for a, b in pairs
        ]

        def enter(pair, real, imag, rows=rows):
            turn_back(states[:2], drop_bit(pair[0], bits[0]), rows, real, imag, *tables(*pair, rows))

        emit(pairs, left, split_ref[...], enter)

    for level, bit in enumerate(bits):
        before = bits[level - 1] if level else None
        after = bits[level + 1] if level + 1 < len(bits) else None
        now, later = states[2 * (level % 2) :][:2], states[2 * ((level + 1) % 2) :][:2]
        for strip in strips:
            rows = slice(strip * half, (strip + 1) * half)
            for was in range(2 if level else 1):
                for will in range(2 if after is not None else 1):
                    chosen, left = [], []
                    for p in range(units // 2):
                        a = spread_index(p, bit)
                        b = a + (1 << bit)
                        if before is not None and (a >> before) & 1 != was:
                            continue
                        if after is not None and (a >> after) & 1 != will:
                            continue
                        chosen.append((a, b))
                        if before is None:
                            left.append(jnp.concatenate([now[0][p, rows], now[1][p, rows]], 1))
                        else:
                            i, j = drop_bit(a, before), drop_bit(b, before)
                            if was:
                                i, j = j, i
                            left.append(
                                jnp.concatenate([jnp.where(low, part[i, rows], part[j, rows]) for part in now], 1)
                            )

                    def leave(pair, real, imag, rows=rows, will=will, bit=bit, after=after, later=later):
                        a, b = pair
                        cosine, sine = tables(b, a, rows) if will else tables(a, b, rows)
                        if after is not None:
                            turn_back(later, drop_bit(a, bit), rows, real, imag, cosine, sine)
                            return
                        for _ in range(3):
                            cosine, sine = cosine * cosine - sine * sine, 2.0 * (cosine * sine)
                        out_ref[a // 2, 0, rows] = (real * cosine - imag * sine).astype(jnp.bfloat16)
                        out_ref[a // 2, 1, rows] = (imag * cosine + real * sine).astype(jnp.bfloat16)

                    emit(chosen, left, (matrix_x, matrix_y)[level % 2][was, will], leave)


def butterfly(values, speed, start, extent, split, matrices, bits, wide=32, strips=STRIPS, group=16):
    sources = values.shape[0]
    size = strips * HALF
    blocks = extent // size
    const = jnp.asarray(trig_constants())
    inputs = [
        pl.BlockSpec((sources, size, 128), lambda g, part=part: (0, part * blocks + g, 0)) for part in range(2)
    ]
    state = pltpu.VMEM((sources, size, 128), jnp.bfloat16)
    table = pltpu.VMEM((2 * sources, size, 128), jnp.float32)
    return pl.pallas_call(
        functools.partial(butterfly_kernel, bits=bits, wide=wide, group=group, start=start),
        grid=(blocks,),
        in_specs=[
            pl.BlockSpec(const.shape, lambda g: (0, 0)),
            pl.BlockSpec(speed.shape, lambda g: (0, 0)),
            pl.BlockSpec(split.shape, lambda g: (0, 0)),
            pl.BlockSpec((2, 2, 256, 256), lambda g: (0, 0, 0, 0)),
            pl.BlockSpec((2, 2, 256, 256), lambda g: (0, 0, 0, 0)),
            *inputs,
        ],
        out_specs=pl.BlockSpec((sources, 2, size, 128), lambda g: (0, 0, g, 0)),
        out_shape=jax.ShapeDtypeStruct((sources, 2, extent, 128), jnp.bfloat16),
        scratch_shapes=[table, table] + [state] * 4,
        compiler_params=pltpu.CompilerParams(vmem_limit_bytes=VMEM_LIMIT),
        cost_estimate=pl.CostEstimate(
            flops=14 * 10**9 * extent // 64, bytes_accessed=8 * 2**20 * extent // 64, transcendentals=0
        ),
    )(const, speed, split, *matrices, values, values)


def finish_kernel(in_ref, *refs):
    out_ref = refs[-1]
    low = lax.broadcasted_iota(jnp.int32, (1, 128), 1) < 64
    for j in range(out_ref.shape[0]):
        real, imag = in_ref[j, 0].astype(jnp.float32), in_ref[j, 1].astype(jnp.float32)
        out_ref[j, 0] = jnp.where(low, real, pltpu.roll(imag, 64, 1))
        out_ref[j, 1] = jnp.where(low, pltpu.roll(real, 64, 1), imag)


def finish(values, chunk, output, group=64):
    boxes, _, extent, _ = values.shape
    earlier = [] if output is None else [output]
    return pl.pallas_call(
        finish_kernel,
        grid=(boxes // group,),
        in_specs=[pl.BlockSpec((group, 2, extent, 128), lambda g: (g, 0, 0, 0))]
        + [pl.BlockSpec(memory_space=pl.ANY)] * len(earlier),
        out_specs=pl.BlockSpec((group, 2, extent, 128), lambda g: (g, 0, chunk, 0)),
        out_shape=jax.ShapeDtypeStruct((boxes, 2, CHUNKS * extent, 128), jnp.float32),
        input_output_aliases={1: 0} if earlier else {},
        compiler_params=pltpu.CompilerParams(vmem_limit_bytes=24 * 2**20),
        cost_estimate=pl.CostEstimate(flops=10**7, bytes_accessed=6 * 2**20, transcendentals=0),
    )(values, *earlier)


def pair_matrices(translation):
    real, imag = translation[:, :, 0], translation[:, :, 1]
    blocks = jnp.stack([jnp.stack([real, imag]), jnp.stack([-imag, real])])
    blocks = blocks.transpose(0, 3, 4, 1, 2, 5)
    rows = jnp.stack([blocks, blocks[:, ::-1]])
    both = jnp.stack([rows, rows[:, :, :, :, :, ::-1]], 1)
    return both.reshape(2, 2, 256, 256)


def split_matrix():
    out = np.zeros((256, 256), np.float32)
    for box in range(2):
        for part in range(2):
            for t in range(64):
                out[box * 128 + part * 64 + t, part * 128 + box * 64 + t] = 1
    return jnp.asarray(out, jnp.bfloat16)


def exchange(values):
    return lax.all_to_all(values, EVERY, 0, 0, tiled=True)


def shards(weights, velocity, translation):
    bits = unit_bits(lax.axis_size("sx"), lax.axis_size("sy"))
    boxes = weights.shape[0]
    size = 64 // CHUNKS
    rows = 2 * size
    split = split_matrix()
    matrices = [pair_matrices(translation[dim]) for dim in range(2)]
    extra = jnp.broadcast_to(velocity[:, None], (boxes, 8, 128))
    first = jnp.concatenate([weights[:, :size], weights[:, 64 : 64 + size], extra], 1)
    first, weights = lax.optimization_barrier((first, weights))
    arrived = [exchange(first)]
    second = jnp.concatenate([weights[:, size:64], weights[:, 64 + size :]], 1)
    arrived[0], second, matrices, split = lax.optimization_barrier((arrived[0], second, matrices, split))
    arrived.append(exchange(second))
    speed = arrived[0][:, rows].astype(jnp.float32)
    back = []
    for chunk in range(CHUNKS):
        done = butterfly(arrived[chunk], speed, chunk * size, size, split, matrices, bits)
        back.append(exchange(done))
    output = None
    for chunk in range(CHUNKS):
        if chunk:
            back[chunk], output = lax.optimization_barrier((back[chunk], output))
        output = finish(back[chunk], chunk, output)
    return output.reshape(weights.shape)


def solution(mesh):
    placed = (P("sx", "sy", None), P("sx", "sy"), P())
    return jax.shard_map(
        shards, mesh=mesh, in_specs=placed, out_specs=P("sx", "sy", None), check_vma=False
    )
```

```python
import functools

import jax
import jax.numpy as jnp
import numpy as np
from jax import lax
from jax.experimental import pallas as pl
from jax.experimental.pallas import tpu as pltpu
from jax.sharding import PartitionSpec as P

TERMS = 7
MAX_ANGLE = 2.95
HALF = 16
EVERY = ("sx", "sy")
CHUNKS = 2
STRIPS = 2
VMEM_LIMIT = 60 * 2**20


def unit_bits(count_x, count_y):
    bits_x = count_x.bit_length() - 1
    bits_y = count_y.bit_length() - 1
    order = []
    for step in range(bits_x):
        order.append(bits_y + bits_x - step)
        order.append(bits_y - step)
    return order


def half_totals():
    counter = np.arange(8, dtype=np.float64)
    nodes = np.cos(np.pi * (2.0 * counter + 1.0) / 16.0)
    totals = (nodes[:, None] + nodes[None, :]).reshape(64) * 0.5
    return np.concatenate([totals, totals])


def trig_constants():
    top = MAX_ANGLE**2
    count = 400
    square = (np.cos(np.pi * (np.arange(count) + 0.5) / count) + 1) / 2 * top
    angle = np.sqrt(square)

    def fit(values):
        series = np.polynomial.chebyshev.Chebyshev.fit(square, values, TERMS - 1, domain=[0, top])
        return series.convert(kind=np.polynomial.Polynomial, domain=[-1, 1], window=[-1, 1]).coef

    rows = np.zeros((TERMS + 1, 128), np.float32)
    rows[:TERMS, :64] = fit(np.cos(angle))[:, None]
    rows[:TERMS, 64:] = fit(np.sin(angle) / angle)[:, None]
    rows[TERMS] = half_totals()
    return rows


def spread_index(place, bit):
    return (place >> bit) << (bit + 1) | place & (1 << bit) - 1


def drop_bit(unit, bit):
    return (unit >> (bit + 1)) << bit | unit & (1 << bit) - 1


def butterfly_kernel(
    const_ref, speed_ref, split_ref, matrix_x, matrix_y, *refs, bits, wide, group, start
):
    in_refs, out_ref, plain_ref, swapped_ref, states = refs[:2], refs[2], refs[3], refs[4], refs[5:]
    sources, extent, _ = in_refs[0].shape
    half = HALF
    strips = range(extent // half)
    units = 2 * sources
    low = lax.broadcasted_iota(jnp.int32, (half, 128), 1) < 64

    first_row = start + pl.program_id(0) * extent
    lane = lax.broadcasted_iota(jnp.int32, (2 * extent * group, 128), 1)
    row = lax.broadcasted_iota(jnp.int32, (2 * extent * group, 128), 0) % (2 * extent)
    diagonal = lane == jnp.where(row < extent, row, row - extent + 64) + first_row
    ones = jnp.ones((128, 128), jnp.bfloat16)

    def trig(index, carry):
        first = index * group
        spread = jnp.concatenate(
            [jnp.broadcast_to(speed_ref[pl.ds(first + j, 1), :], (2 * extent, 128)) for j in range(group)], 0
        )
        picked = jnp.where(diagonal, spread, 0.0).astype(jnp.bfloat16)
        speed = jnp.dot(picked, ones, preferred_element_type=jnp.float32)
        angle = speed * const_ref[TERMS : TERMS + 1, :]
        square = angle * angle
        series = jnp.broadcast_to(const_ref[TERMS - 1 : TERMS, :], square.shape)
        for k in range(TERMS - 2, -1, -1):
            series = series * square + const_ref[k : k + 1, :]
        both = series * jnp.where(lane < 64, 1.0, angle)
        plain_ref[pl.ds(2 * first, 2 * group)] = both.reshape(2 * group, extent, 128)
        swapped_ref[pl.ds(2 * first, 2 * group)] = pltpu.roll(both, 64, 1).reshape(2 * group, extent, 128)
        return carry

    lax.fori_loop(0, units // 2 // group, trig, 0)

    def tables(first, second, rows):
        cosine = jnp.where(low, plain_ref[first, rows], swapped_ref[second, rows])
        sine = jnp.where(low, swapped_ref[first, rows], plain_ref[second, rows])
        return cosine, sine

    def emit(chosen, left, matrix, finish):
        for begin in range(0, len(chosen), wide):
            joined = jnp.dot(
                jnp.concatenate(left[begin : begin + wide], 0), matrix, preferred_element_type=jnp.float32
            )
            for k, pair in enumerate(chosen[begin : begin + wide]):
                part = joined[k * half : (k + 1) * half]
                finish(pair, part[:, :128], part[:, 128:])

    def turn_back(target, place, rows, real, imag, cosine, sine):
        re_ref, im_ref = target
        re_ref[place, rows] = (real * cosine + imag * sine).astype(jnp.bfloat16)
        im_ref[place, rows] = (imag * cosine - real * sine).astype(jnp.bfloat16)

    pairs = [(spread_index(p, bits[0]), spread_index(p, bits[0]) + (1 << bits[0])) for p in range(units // 2)]
    for strip in strips:
        rows = slice(strip * half, (strip + 1) * half)
        left = [
            jnp.concatenate([in_refs[a % 2][a // 2, rows], in_refs[b % 2][b // 2, rows]], 1) for a, b in pairs
        ]

        def enter(pair, real, imag, rows=rows):
            turn_back(states[:2], drop_bit(pair[0], bits[0]), rows, real, imag, *tables(*pair, rows))

        emit(pairs, left, split_ref[...], enter)

    for level, bit in enumerate(bits):
        before = bits[level - 1] if level else None
        after = bits[level + 1] if level + 1 < len(bits) else None
        now, later = states[2 * (level % 2) :][:2], states[2 * ((level + 1) % 2) :][:2]
        for strip in strips:
            rows = slice(strip * half, (strip + 1) * half)
            for was in range(2 if level else 1):
                for will in range(2 if after is not None else 1):
                    chosen, left = [], []
                    for p in range(units // 2):
                        a = spread_index(p, bit)
                        b = a + (1 << bit)
                        if before is not None and (a >> before) & 1 != was:
                            continue
                        if after is not None and (a >> after) & 1 != will:
                            continue
                        chosen.append((a, b))
                        if before is None:
                            left.append(jnp.concatenate([now[0][p, rows], now[1][p, rows]], 1))
                        else:
                            i, j = drop_bit(a, before), drop_bit(b, before)
                            if was:
                                i, j = j, i
                            left.append(
                                jnp.concatenate([jnp.where(low, part[i, rows], part[j, rows]) for part in now], 1)
                            )

                    def leave(pair, real, imag, rows=rows, will=will, bit=bit, after=after, later=later):
                        a, b = pair
                        cosine, sine = tables(b, a, rows) if will else tables(a, b, rows)
                        if after is not None:
                            turn_back(later, drop_bit(a, bit), rows, real, imag, cosine, sine)
                            return
                        for _ in range(3):
                            cosine, sine = cosine * cosine - sine * sine, 2.0 * (cosine * sine)
                        out_ref[a // 2, 0, rows] = (real * cosine - imag * sine).astype(jnp.bfloat16)
                        out_ref[a // 2, 1, rows] = (imag * cosine + real * sine).astype(jnp.bfloat16)

                    emit(chosen, left, (matrix_x, matrix_y)[level % 2][was, will], leave)


def butterfly(values, speed, start, extent, split, matrices, bits, wide=32, strips=STRIPS, group=16):
    sources = values.shape[0]
    size = strips * HALF
    blocks = extent // size
    const = jnp.asarray(trig_constants())
    inputs = [
        pl.BlockSpec((sources, size, 128), lambda g, part=part: (0, part * blocks + g, 0)) for part in range(2)
    ]
    state = pltpu.VMEM((sources, size, 128), jnp.bfloat16)
    table = pltpu.VMEM((2 * sources, size, 128), jnp.float32)
    return pl.pallas_call(
        functools.partial(butterfly_kernel, bits=bits, wide=wide, group=group, start=start),
        grid=(blocks,),
        in_specs=[
            pl.BlockSpec(const.shape, lambda g: (0, 0)),
            pl.BlockSpec(speed.shape, lambda g: (0, 0)),
            pl.BlockSpec(split.shape, lambda g: (0, 0)),
            pl.BlockSpec((2, 2, 256, 256), lambda g: (0, 0, 0, 0)),
            pl.BlockSpec((2, 2, 256, 256), lambda g: (0, 0, 0, 0)),
            *inputs,
        ],
        out_specs=pl.BlockSpec((sources, 2, size, 128), lambda g: (0, 0, g, 0)),
        out_shape=jax.ShapeDtypeStruct((sources, 2, extent, 128), jnp.bfloat16),
        scratch_shapes=[table, table] + [state] * 4,
        compiler_params=pltpu.CompilerParams(vmem_limit_bytes=VMEM_LIMIT),
        cost_estimate=pl.CostEstimate(
            flops=14 * 10**9 * extent // 64, bytes_accessed=8 * 2**20 * extent // 64, transcendentals=0
        ),
    )(const, speed, split, *matrices, values, values)


def finish_kernel(in_ref, *refs):
    out_ref = refs[-1]
    low = lax.broadcasted_iota(jnp.int32, (1, 128), 1) < 64
    for j in range(out_ref.shape[0]):
        real, imag = in_ref[j, 0].astype(jnp.float32), in_ref[j, 1].astype(jnp.float32)
        out_ref[j, 0] = jnp.where(low, real, pltpu.roll(imag, 64, 1))
        out_ref[j, 1] = jnp.where(low, pltpu.roll(real, 64, 1), imag)


def finish(values, chunk, output, group=64):
    boxes, _, extent, _ = values.shape
    earlier = [] if output is None else [output]
    return pl.pallas_call(
        finish_kernel,
        grid=(boxes // group,),
        in_specs=[pl.BlockSpec((group, 2, extent, 128), lambda g: (g, 0, 0, 0))]
        + [pl.BlockSpec(memory_space=pl.ANY)] * len(earlier),
        out_specs=pl.BlockSpec((group, 2, extent, 128), lambda g: (g, 0, chunk, 0)),
        out_shape=jax.ShapeDtypeStruct((boxes, 2, CHUNKS * extent, 128), jnp.float32),
        input_output_aliases={1: 0} if earlier else {},
        compiler_params=pltpu.CompilerParams(vmem_limit_bytes=24 * 2**20),
        cost_estimate=pl.CostEstimate(flops=10**7, bytes_accessed=6 * 2**20, transcendentals=0),
    )(values, *earlier)


def pair_matrices(translation):
    real, imag = translation[:, :, 0], translation[:, :, 1]
    blocks = jnp.stack([jnp.stack([real, imag]), jnp.stack([-imag, real])])
    blocks = blocks.transpose(0, 3, 4, 1, 2, 5)
    rows = jnp.stack([blocks, blocks[:, ::-1]])
    both = jnp.stack([rows, rows[:, :, :, :, :, ::-1]], 1)
    return both.reshape(2, 2, 256, 256)


def split_matrix():
    out = np.zeros((256, 256), np.float32)
    for box in range(2):
        for part in range(2):
            for t in range(64):
                out[box * 128 + part * 64 + t, part * 128 + box * 64 + t] = 1
    return jnp.asarray(out, jnp.bfloat16)


def exchange(values):
    return lax.all_to_all(values, EVERY, 0, 0, tiled=True)


def shards(weights, velocity, translation):
    bits = unit_bits(lax.axis_size("sx"), lax.axis_size("sy"))
    boxes = weights.shape[0]
    size = 64 // CHUNKS
    rows = 2 * size
    split = split_matrix()
    matrices = [pair_matrices(translation[dim]) for dim in range(2)]
    first = jnp.concatenate([weights[:, :size], weights[:, 64 : 64 + size + 8]], 1)
    first = jnp.where(lax.broadcasted_iota(jnp.int32, first.shape, 1) < rows, first, velocity[:, None])
    first, weights = lax.optimization_barrier((first, weights))
    arrived = [exchange(first)]
    second = jnp.concatenate([weights[:, size:64], weights[:, 64 + size :]], 1)
    arrived[0], second, matrices, split = lax.optimization_barrier((arrived[0], second, matrices, split))
    arrived.append(exchange(second))
    speed = arrived[0][:, rows].astype(jnp.float32)
    back = []
    for chunk in range(CHUNKS):
        done = butterfly(arrived[chunk], speed, chunk * size, size, split, matrices, bits)
        back.append(exchange(done))
    output = None
    for chunk in range(CHUNKS):
        if chunk:
            back[chunk], output = lax.optimization_barrier((back[chunk], output))
        output = finish(back[chunk], chunk, output)
    return output.reshape(weights.shape)


def solution(mesh):
    placed = (P("sx", "sy", None), P("sx", "sy"), P())
    return jax.shard_map(
        shards, mesh=mesh, in_specs=placed, out_specs=P("sx", "sy", None), check_vma=False
    )
```
